512 devices in a mesh: member: 16 (over z_hi, y, core), tensor: 32 (over z_lo, x).
Axes of the slice: x: 4, y: 4, z: 16 (z_hi: 2, z_lo: 8; z = z_hi * 8 + z_lo), core: 2. Of those that a mesh axis runs over, the one named last changes fastest.
Arguments:
- layer_input: bfloat16 [16, 4096, 8192], P('member', 'tensor'), may hold values from -6 to 6
- value_grads: bfloat16 [16, 4096, 1024], P('member', 'tensor'), may hold values from -6 to 6
- value_weight: bfloat16 [8192, 1024], P('tensor', 'member'), may hold values from -0.0625 to 0.0625
- adapter_down: bfloat16 [16, 8192, 64], P('member', 'tensor'), may hold values from -0.0625 to 0.0625
- adapter_up: bfloat16 [16, 64, 1024], P('member'), may hold values from -0.1875 to 0.1875
- norm_gain: float32 [8192], replicated, may hold values from 0.1 to 1.9
Outputs:
- input_grads: bfloat16 [16, 4096, 8192], P('member', 'tensor')
- down_grads: float32 [16, 8192, 64], P('member', 'tensor')
- up_grads: float32 [16, 64, 1024], P('member', None, 'tensor')
The draws below stay inside these ranges and needn't reach their ends.
All inputs are finite; a program needn't handle non-finite values.
Results may differ from the reference program's by a relative error of at most 0.0054.
Values may be sent and summed in bfloat16 or wider, within the bound.
A program may use at most 64 MiB of HBM per device.

```python
import math
import jax
import jax.numpy as jnp
from jax import lax

D = 8192
KV = 1024
R = 64
MEMBER_TOKENS = 4096
MEMBERS = 16


def strengthened(result, own_key, source, target, blocks, factor):
    def block_of(position):
        return (jnp.arange(result.shape[position]) // (result.shape[position] // blocks)).reshape((-1,) + (1,) * (result.ndim - 1 - position))

    first = jax.random.permutation(own_key, blocks)[block_of(target)]
    second = (block_of(target) + blocks // 2) % blocks
    return jnp.where((block_of(source) == first) | (block_of(source) == second), factor * result, result)


def levels(own_key, extent, split, low, largest):
    def one(position, parts):
        heights = jax.random.uniform(jax.random.fold_in(jax.random.fold_in(own_key, 6), position), (parts,), jnp.float32, low / len(split), largest / len(split))
        return jnp.repeat(jnp.exp(heights), extent[position] // parts).reshape((-1,) + (1,) * (len(extent) - position - 1))

    level = one(*split[0])
    for cut in split[1:]:
        level = level * one(*cut)
    return level


def noise(key, extent, deviation, reach, shards=(), kind=jnp.bfloat16):
    drawn = deviation * jax.random.normal(key, extent, jnp.float32)
    if shards:
        drawn = drawn * levels(key, extent, shards, -0.22, 0.18)
    return jnp.clip(drawn, -reach, reach).astype(kind)


def bell_draw_with(own_key, dims, deviation, most, split, heavy, held_as=jnp.bfloat16):
    array = deviation * jax.random.normal(own_key, dims, jnp.float32)
    if split:
        array = array * levels(own_key, dims, split, -0.22, 0.18)
    return jnp.clip(strengthened(array, jax.random.fold_in(own_key, 3), *heavy), -most, most).astype(held_as)


def setup_inputs(seed: int = 0) -> dict:
    splits = jax.random.split(jax.random.key(seed), 7)
    layer_input = bell_draw_with(splits[0], (MEMBERS, MEMBER_TOKENS, D), 1.0, 6.0, ((0, 16), (1, 32)), (1, 2, 32, 2.75))
    value_grads = noise(splits[1], (MEMBERS, MEMBER_TOKENS, KV), 1.0, 6.0, ((0, 16), (1, 32)))
    value_weight = noise(splits[2], (D, KV), D ** -0.5, 0.0625, ((0, 32), (1, 16)))
    adapter_down = noise(splits[3], (MEMBERS, D, R), D ** -0.5, 0.0625, ((0, 16), (1, 32)))
    adapter_up = noise(splits[4], (MEMBERS, R, KV), KV ** -0.5, 0.1875, ((0, 16),))
    norm_gain = jnp.clip(1.0 + 0.18 * jax.random.normal(splits[5], (D,), jnp.float32), 0.1, 1.9)
    return {"layer_input": layer_input, "value_grads": value_grads, "value_weight": value_weight, "adapter_down": adapter_down, "adapter_up": adapter_up, "norm_gain": norm_gain}


adapter_scale = 4.0
gradient_scale = 1.0
norm_eps = 1e-05

def one_member(pieces, value_weight, norm_gain):
    layer_input, value_grads, adapter_down, adapter_up = pieces
    widened = layer_input.astype(jnp.float32)
    inverse_rms = lax.rsqrt(lax.optimization_barrier(jnp.mean(widened * widened, axis=-1, keepdims=True)) + norm_eps)
    normed = widened * inverse_rms
    scaled = (normed * norm_gain).astype(jnp.bfloat16)
    lowrank_grad = jnp.dot(value_grads, adapter_up.T, preferred_element_type=jnp.float32).astype(jnp.bfloat16)
    frozen_product = jnp.dot(value_grads, value_weight.T, preferred_element_type=jnp.float32)
    adapter_product = jnp.dot(lowrank_grad, adapter_down.T, preferred_element_type=jnp.float32)
    feature_gradient = (frozen_product + adapter_scale * adapter_product).astype(jnp.bfloat16)
    gained = norm_gain * feature_gradient.astype(jnp.float32)
    center = lax.optimization_barrier(jnp.mean(gained * normed, axis=-1, keepdims=True))
    input_grads = (inverse_rms * (gained - normed * center)).astype(jnp.bfloat16)
    lowrank_in = jnp.dot(scaled, adapter_down, preferred_element_type=jnp.float32).astype(jnp.bfloat16)
    scaling_multiplier = gradient_scale / math.sqrt(MEMBER_TOKENS)
    down_grads = scaling_multiplier * jnp.dot(scaled.T, lowrank_grad, preferred_element_type=jnp.float32)
    up_grads = scaling_multiplier * jnp.dot(lowrank_in.T, value_grads, preferred_element_type=jnp.float32)
    return (input_grads, down_grads, up_grads)

def reference(layer_input, value_grads, value_weight, adapter_down, adapter_up, norm_gain):

    def member_step(pieces):
        return one_member(pieces, value_weight, norm_gain)
    input_grads, down_grads, up_grads = lax.map(member_step, (layer_input, value_grads, adapter_down, adapter_up))
    return (input_grads, down_grads, up_grads)
```

```python
import functools
import math

import jax
import jax.numpy as jnp
from jax import lax
from jax.experimental import pallas as pl
from jax.experimental.pallas import tpu as pltpu
from jax.sharding import PartitionSpec as P

adapter_scale = 4.0
gradient_scale = 1.0
norm_eps = 1e-05

F32 = jnp.float32
BF16 = jnp.bfloat16
MESH = pl.DeviceIdType.MESH
ZL, ZH, NX, NY = 8, 2, 4, 4
NZ = ZL * ZH
D = 8192
KV = 1024
R = 64
T = 128
B = 256
NN = (((1,), (0,)), ((), ()))
NT = (((1,), (1,)), ((), ()))
TN = (((0,), (0,)), ((), ()))


def dot(a, b, dims):
    return lax.dot_general(a, b, dims, preferred_element_type=F32)


def mod(a, n):
    return lax.rem(a + 4 * n, n)


def main_kernel(
    x_hbm, grads, w_in, d_in, up, gain,
    fg, down_out, up_out,
    xv, scaled, buf, dbuf, tok, lr4, res, inv,
    part, part_in, summed, chain, lin, upart, upart_in, usum, uin,
    s_loc, s_w2, s_g, s_z, s_y1, s_y2, s_sib, s_d, s_p, s_c, s_res, s_own, s_u, s_uz,
):
    m = lax.axis_index("member")
    t = lax.axis_index("tensor")
    zh, y, c = m // 8, (m // 2) % 4, m % 2
    zl, xx = t // 4, t % 4
    z = zh * ZL + zl
    par, xs = xx % 2, xx // 2
    sib_c = 1 - c

    def dev(z_, y_, x_, c_):
        return ((z_ // ZL) * 8 + y_ * 2 + c_, (z_ % ZL) * 4 + x_)

    zp, zm = dev(mod(z + 1, NZ), y, xx, c), dev(mod(z - 1, NZ), y, xx, c)
    yp, ym = dev(z, mod(y + 1, NY), xx, c), dev(z, mod(y - 1, NY), xx, c)
    sib = dev(z, y, xx, sib_c)

    def xdev(d):
        return dev(z, y, mod(xx + d, NX), c)

    def remote(src, dst, sems, idx, target):
        return pltpu.make_async_remote_copy(
            src_ref=src, dst_ref=dst, send_sem=sems.at[(0,) + idx],
            recv_sem=sems.at[(1,) + idx], device_id=target, device_id_type=MESH,
        )

    sends = []

    def start(src, dst, sems, idx, target):
        cp = remote(src, dst, sems, idx, target)
        cp.start()
        sends.append(cp)

    def arrived(ref, sems, idx):
        remote(ref, ref, sems, idx, sib).wait_recv()

    load_x = pltpu.make_async_copy(x_hbm, xv, s_loc)
    load_x.start()

    barrier = pltpu.get_barrier_semaphore()
    for peer in (zp, zm, yp, ym, xdev(1), xdev(2), xdev(3), sib):
        pl.semaphore_signal(barrier, inc=1, device_id=peer, device_id_type=MESH)

    eye = (
        lax.broadcasted_iota(jnp.int32, (R, R), 0) == lax.broadcasted_iota(jnp.int32, (R, R), 1)
    ).astype(BF16)

    def piece(zsrc, parts, ysrc, csrc):
        return buf.at[parts, zsrc % ZL, zsrc // ZL, ysrc, csrc]

    buf[xs, zl, zh, y, c] = dot(eye, w_in[...], NT).astype(BF16)
    dt_own = dot(eye, d_in[...], NT).astype(BF16)
    buf[2, zl, zh, y, c] = dt_own
    dbuf[zl, xx] = dt_own
    pl.semaphore_wait(barrier, 8)

    start(piece(z, xs, y, c), piece(z, xs, y, c), s_w2, (), xdev(2))
    tok[0:T] = grads[...]
    start(grads.at[0:64], tok.at[128:192], s_g, (0,), xdev(1))
    start(grads.at[64:128], tok.at[192:256], s_g, (1,), xdev(3))

    lr_own = dot(grads[...], up[...], NT).astype(BF16)
    lr_t = dot(up[...], grads[...], NT).astype(BF16)
    lr4[0:T] = lr_own * adapter_scale

    load_x.wait()

    def square(i, acc):
        v = xv[:, pl.ds(pl.multiple_of(i * B, B), B)].astype(F32)
        return acc + v * v

    total = lax.fori_loop(0, 32, square, jnp.zeros((T, B), F32))
    inv[...] = lax.rsqrt(jnp.sum(total, axis=1, keepdims=True) / D + norm_eps)

    arrived(piece(z, 1 - xs, y, c), s_w2, ())

    def source(q):
        steps = (q + 1) // 2
        return mod(z - steps, NZ) if q % 2 else mod(z + steps, NZ)

    def of_step(s):
        return [0] if s == 0 else ([15] if s == 8 else [2 * s - 1, 2 * s])

    def z_parts(s, direction):
        return pl.ds(0, 3) if s < 8 else (0 if direction == 0 else 1)

    def z_send(s):
        up_src, down_src = mod(z - s + 1, NZ), mod(z + s - 1, NZ)
        a = piece(up_src, z_parts(s, 0), y, c)
        b = piece(down_src, z_parts(s, 1), y, c)
        start(a, a, s_z, (0, s), zp)
        start(b, b, s_z, (1, s), zm)

    def z_wait(s):
        arrived(piece(mod(z - s, NZ), z_parts(s, 0), y, c), s_z, (0, s))
        arrived(piece(mod(z + s, NZ), z_parts(s, 1), y, c), s_z, (1, s))

    both = pl.ds(0, 2)

    def y_send(q):
        src = piece(source(q), both, y, c)
        start(src, src, s_y1, (0, q), yp)
        start(src, src, s_y1, (1, q), ym)

    def y_relay(q):
        below, above = mod(y - 1, NY), mod(y + 1, NY)
        arrived(piece(source(q), both, below, c), s_y1, (0, q))
        src = piece(source(q), 0, below, c)
        start(src, src, s_y2, (0, q), yp)
        arrived(piece(source(q), both, above, c), s_y1, (1, q))
        src = piece(source(q), 1, above, c)
        start(src, src, s_y2, (1, q), ym)

    def y_done(q):
        far = mod(y + 2, NY)
        arrived(piece(source(q), 0, far, c), s_y2, (0, q))
        arrived(piece(source(q), 1, far, c), s_y2, (1, q))
        src = piece(source(q), both, slice(None), c)
        start(src, src, s_sib, (q,), sib)

    def sib_done(q):
        arrived(piece(source(q), both, slice(None), sib_c), s_sib, (q,))

    def in_line(s, direction):
        return zl >= s if direction == 0 else zl + s < ZL

    def d_send(s):
        for direction in (0, 1) if s else (0,):
            row = zl - s if direction == 0 else zl + s

            def go(row=row):
                src = buf.at[2, row, zh, y, c]
                if s:
                    dbuf[row, xx] = src[...]
                for d in (1, 2, 3):
                    remote(src, dbuf.at[row, xx], s_d, (d, row), xdev(d)).start()

            pl.when(in_line(s, direction))(go)

    def d_done(s):
        for direction in (0, 1) if s else (0,):
            row = zl - s if direction == 0 else zl + s

            def go(row=row):
                for d in (1, 2, 3):
                    remote(dbuf.at[row, xx], dbuf.at[row, mod(xx - d, NX)], s_d, (d, row), sib).wait()

                def add(i, acc):
                    return acc + dot(scaled[row * 4 + i], dbuf[row, i], NT)

                lin[...] += lax.fori_loop(0, 4, add, jnp.zeros((T, R), F32))

            pl.when(in_line(s, direction))(go)

    def rows_of(j):
        if j == 8:
            return [(True, zl)]
        return [(zl + 8 - j < ZL, zl + 8 - j), (zl - 8 + j >= 0, zl - 8 + j)]

    def p_send(j):
        for ok, row in rows_of(j):

            def go(row=row):
                def one(i, carry):
                    part[i, row] = dot(lr_t, scaled[row * 4 + i], NN).astype(BF16)
                    return carry

                lax.fori_loop(0, 4, one, 0)
                for d in (1, 2, 3):
                    remote(
                        part.at[mod(xx + d, NX), row], part_in.at[d, row], s_p, (d, row), xdev(d)
                    ).start()

            if ok is True:
                go()
            else:
                pl.when(ok)(go)

    def p_done(j):
        for ok, row in rows_of(j):

            def go(row=row):
                acc = part[xx, row].astype(F32)
                for d in (1, 2, 3):
                    remote(
                        part.at[mod(xx + d, NX), row], part_in.at[d, row], s_p, (d, row), sib
                    ).wait()
                    acc += part_in[d, row].astype(F32)
                summed[row] = acc

            if ok is True:
                go()
            else:
                pl.when(ok)(go)

    def c_step(j):
        for direction, place, peer, row in (
            (0, zl, zp, zl + 8 - j), (1, 7 - zl, zm, zl - 8 + j)
        ):
            if j <= 7:

                def first(direction=direction, peer=peer, row=row):
                    remote(
                        summed.at[row], chain.at[direction, j], s_c, (direction, j), peer
                    ).start()

                pl.when(place == 0)(first)
                if j >= 2:

                    def later(direction=direction, peer=peer, row=row):
                        arrived(chain.at[direction, j - 1], s_c, (direction, j - 1))
                        chain[direction, j - 1] += summed[row]
                        remote(
                            chain.at[direction, j - 1], chain.at[direction, j], s_c,
                            (direction, j), peer,
                        ).start()

                    pl.when((place >= 1) & (place <= j - 1))(later)

    def c_last():
        down_out[...] = summed[zl]
        for direction, place in ((0, zl), (1, 7 - zl)):

            def go(direction=direction):
                arrived(chain.at[direction, 7], s_c, (direction, 7))
                down_out[...] += chain[direction, 7]

            pl.when(place >= 1)(go)

    def block(row):
        def one(i, carry):
            w = buf[i, row].reshape(KV, B)
            acc = dot(tok[...], w, NN) + dot(lr4[...], dbuf[row, par + 2 * i], NN)
            res[row, i] = acc.astype(BF16)
            return carry

        lax.fori_loop(0, 2, one, 0)
        remote(
            res.at[row, :, 128:192], fg.at[row, :, par, 0:64], s_res, (0, row), xdev(3)
        ).start()
        remote(
            res.at[row, :, 192:256], fg.at[row, :, par, 64:128], s_res, (1, row), xdev(1)
        ).start()
        pltpu.make_async_copy(res.at[row, :, 0:128], fg.at[row, :, par], s_own.at[row]).start()

    def finished(s):
        if s < 4:
            return []
        if s == 4:
            return [mod(zl + 4, ZL)]
        if s == 8:
            return [zl]
        return [mod(zl + s, ZL), mod(zl - s, ZL)]

    def pack_up():
        lb = lin[...].astype(BF16)
        term = dot(grads[...], lb, TN)
        upart[...] = term.reshape(ZL, NX, 32, R).swapaxes(0, 1).astype(BF16)
        for d in (1, 2, 3):
            start(upart.at[mod(xx + d, NX)], upart_in.at[d], s_u, (d,), xdev(d))

    def up_over_z():
        acc = upart[xx].astype(F32)
        for d in (1, 2, 3):
            arrived(upart_in.at[d], s_u, (d,))
            acc += upart_in[d].astype(F32)
        usum[...] = acc
        for d in range(1, 8):
            row = mod(zl + d, ZL)
            start(usum.at[row], uin.at[d], s_uz, (d,), dev(zh * ZL + row, y, xx, c))

    def up_last():
        acc = usum[zl]
        for d in range(1, 8):
            arrived(uin.at[d], s_uz, (d,))
            acc += uin[d]
        up_out[...] = acc

    def make_scaled(i, carry):
        v = xv[:, pl.ds(pl.multiple_of(i * B, B), B)].astype(F32)
        scaled[i] = (v * inv[...] * gain[pl.ds(i, 1), :]).astype(BF16)
        return carry

    lin[...] = jnp.zeros_like(lin)
    for s in range(0, 12):
        if 1 <= s <= 8:
            z_wait(s)
        if s <= 7:
            z_send(s + 1)
        if s <= 8:
            for q in of_step(s):
                y_send(q)
        if s <= 7:
            d_send(s)
        if s == 0:
            lax.fori_loop(0, 32, make_scaled, 0)
        if 1 <= s <= 8:
            p_send(s)
        if 0 <= s - 1 <= 8:
            for q in of_step(s - 1):
                y_relay(q)
        if s == 1:
            arrived(tok.at[128:192], s_g, (0,))
            arrived(tok.at[192:256], s_g, (1,))
            lr4[T:] = dot(tok[T:], up[...], NT).astype(BF16) * adapter_scale
        if 0 <= s - 2 <= 7:
            p_done(s - 1)
        if 1 <= s - 2 <= 7:
            c_step(s - 2)
        if 0 <= s - 1 <= 7:
            d_done(s - 1)
        if s == 8:
            pack_up()
        if s == 10:
            up_over_z()
        if 0 <= s - 2 <= 8:
            for q in of_step(s - 2):
                y_done(q)
        if 0 <= s - 3 <= 8:
            for q in of_step(s - 3):
                sib_done(q)
            for row in finished(s - 3):
                block(row)

    c_last()
    up_last()
    for row in range(ZL):
        pltpu.make_async_copy(res.at[row, :, 0:128], fg.at[row, :, par], s_own.at[row]).wait()
        remote(
            res.at[row, :, 128:192], fg.at[row, :, 1 - par, 0:64], s_res, (0, row), sib
        ).wait()
        remote(
            res.at[row, :, 192:256], fg.at[row, :, 1 - par, 64:128], s_res, (1, row), sib
        ).wait()
    for j in range(1, 8):
        for direction, place in ((0, zl), (1, 7 - zl)):

            def go(direction=direction, j=j):
                remote(summed.at[0], chain.at[direction, j], s_c, (direction, j), sib).wait_send()

            pl.when(place <= j - 1)(go)
    for cp in sends:
        cp.wait_send()


def exchange(x, grads, w, d, up, gain):
    sem = pltpu.SemaphoreType.DMA
    vmem = pl.BlockSpec(memory_space=pltpu.VMEM)
    hbm = pl.BlockSpec(memory_space=pl.ANY)
    return pl.pallas_call(
        main_kernel,
        out_shape=(
            jax.ShapeDtypeStruct((ZL, 2, 2, T, B), BF16),
            jax.ShapeDtypeStruct((R, B), F32),
            jax.ShapeDtypeStruct((32, R), F32),
        ),
        in_specs=[hbm, vmem, vmem, vmem, vmem, vmem],
        out_specs=(hbm, vmem, vmem),
        scratch_shapes=[
            pltpu.VMEM((T, D), BF16),
            pltpu.VMEM((32, T, B), BF16),
            pltpu.VMEM((3, ZL, ZH, NY, 2, R, B), BF16),
            pltpu.VMEM((ZL, NX, R, B), BF16),
            pltpu.VMEM((2 * T, KV), BF16),
            pltpu.VMEM((2 * T, R), BF16),
            pltpu.VMEM((ZL, 2, 2 * T, B), BF16),
            pltpu.VMEM((T, 1), F32),
            pltpu.VMEM((NX, ZL, R, B), BF16),
            pltpu.VMEM((NX, ZL, R, B), BF16),
            pltpu.VMEM((ZL, R, B), F32),
            pltpu.VMEM((2, 8, R, B), F32),
            pltpu.VMEM((T, R), F32),
            pltpu.VMEM((NX, ZL, 32, R), BF16),
            pltpu.VMEM((NX, ZL, 32, R), BF16),
            pltpu.VMEM((ZL, 32, R), F32),
            pltpu.VMEM((ZL, 32, R), F32),
            sem,
            sem((2,)),
            sem((2, 2)),
            sem((2, 2, 9)),
            sem((2, 2, 16)),
            sem((2, 2, 16)),
            sem((2, 16)),
            sem((2, 4, 8)),
            sem((2, 4, 8)),
            sem((2, 2, 8)),
            sem((2, 2, 8)),
            sem((8,)),
            sem((2, 4)),
            sem((2, 8)),
        ],
        compiler_params=pltpu.CompilerParams(
            collective_id=1, has_side_effects=True, vmem_limit_bytes=50 << 20
        ),
        name="exchange",
    )(x, grads, w, d, up, gain)


def finish_kernel(x, fg, gain, out):
    rows = x.shape[0]
    squares = jnp.zeros((rows, B), F32)
    products = jnp.zeros((rows, B), F32)
    for i in range(32):
        v = x[:, i * B:(i + 1) * B].astype(F32)
        g = fg[i // 4, (i % 4) // 2, i % 2].astype(F32) * gain[i:i + 1, :]
        squares += v * v
        products += v * g
    inv = lax.rsqrt(jnp.sum(squares, axis=1, keepdims=True) / D + norm_eps)
    slope = inv * inv * (jnp.sum(products, axis=1, keepdims=True) / D)
    for i in range(32):
        v = x[:, i * B:(i + 1) * B].astype(F32)
        g = fg[i // 4, (i % 4) // 2, i % 2].astype(F32) * gain[i:i + 1, :]
        out[:, i * B:(i + 1) * B] = (inv * (g - v * slope)).astype(BF16)


def finish(x, fg, gain):
    rows = 32
    return pl.pallas_call(
        finish_kernel,
        grid=(T // rows,),
        out_shape=jax.ShapeDtypeStruct((T, D), BF16),
        in_specs=[
            pl.BlockSpec((rows, D), lambda i: (i, 0)),
            pl.BlockSpec((ZL, 2, 2, rows, B), lambda i: (0, 0, 0, i, 0)),
            pl.BlockSpec((32, B), lambda i: (0, 0)),
        ],
        out_specs=pl.BlockSpec((rows, D), lambda i: (i, 0)),
        compiler_params=pltpu.CompilerParams(vmem_limit_bytes=32 << 20),
        name="finish",
    )(x, fg, gain)


def per_device(layer_input, value_grads, value_weight, adapter_down, adapter_up, norm_gain):
    scaling = gradient_scale / math.sqrt(layer_input.shape[1] * lax.axis_size("tensor"))
    gain = norm_gain.reshape(32, B)
    fg, down_t, up_t = exchange(
        layer_input[0], value_grads[0], value_weight, adapter_down[0], adapter_up[0], gain
    )
    input_grads = finish(layer_input[0], fg, gain)
    return (input_grads[None], (scaling * down_t.T)[None], (scaling * up_t.T)[None])


def solution(mesh):
    return jax.shard_map(
        per_device,
        mesh=mesh,
        in_specs=(
            P("member", "tensor", None),
            P("member", "tensor", None),
            P("tensor", "member"),
            P("member", "tensor", None),
            P("member", None, None),
            P(),
        ),
        out_specs=(
            P("member", "tensor", None),
            P("member", "tensor", None),
            P("member", None, "tensor"),
        ),
        check_vma=False,
    )
```

```python
import functools
import math

import jax
import jax.numpy as jnp
from jax import lax
from jax.experimental import pallas as pl
from jax.experimental.pallas import tpu as pltpu
from jax.sharding import PartitionSpec as P

adapter_scale = 4.0
gradient_scale = 1.0
norm_eps = 1e-05

F32 = jnp.float32
BF16 = jnp.bfloat16
MESH = pl.DeviceIdType.MESH
ZL, ZH, NX, NY = 8, 2, 4, 4
NZ = ZL * ZH
D = 8192
KV = 1024
R = 64
T = 128
B = 256
NN = (((1,), (0,)), ((), ()))
NT = (((1,), (1,)), ((), ()))
TN = (((0,), (0,)), ((), ()))


def dot(a, b, dims):
    return lax.dot_general(a, b, dims, preferred_element_type=F32)


def mod(a, n):
    return lax.rem(a + 4 * n, n)


def main_kernel(
    x_hbm, grads_hbm, w_hbm, d_hbm, up_hbm, gain_hbm,
    fg, down_out, up_out,
    xv, raw, up, up2, gain, scaled, buf, dbuf, tok, lr4, res, inv,
    part, part_in, summed, chain, lin, upart, upart_in, usum, uin,
    down, upg, s_loc, s_send, r_one, r_z, r_z8, r_dz, r_y1, r_y2, r_sib, r_d, r_p, r_c, r_res,
):
    m = lax.axis_index("member")
    t = lax.axis_index("tensor")
    zh, y, c = m // 8, (m // 2) % 4, m % 2
    zl, xx = t // 4, t % 4
    z = zh * ZL + zl
    par, xs = xx % 2, xx // 2

    def dev(z_, y_, x_, c_):
        return ((z_ // ZL) * 8 + y_ * 2 + c_, (z_ % ZL) * 4 + x_)

    y_up, y_down, y_far = mod(y + 1, NY), mod(y - 1, NY), mod(y + 2, NY)
    zp, zm = dev(mod(z + 1, NZ), y, xx, c), dev(mod(z - 1, NZ), y, xx, c)
    yp, ym, yf = dev(z, y_up, xx, c), dev(z, y_down, xx, c), dev(z, y_far, xx, c)
    sib = dev(z, y, xx, 1 - c)
    xpeer = {d: dev(z, y, mod(xx + d, NX), c) for d in (1, 2, 3)}

    (w2, g_, z_, y1, y2, sb, d_, p_, res_, u_, uz, own_, dz0, dz1, c0, c1) = [
        s_send.at[i] for i in range(16)
    ]
    r_w2, r_g, r_u, r_uz = [r_one.at[i] for i in range(4)]

    def remote(src, dst, sent, got, target):
        return pltpu.make_async_remote_copy(
            src_ref=src, dst_ref=dst, send_sem=sent, recv_sem=got,
            device_id=target, device_id_type=MESH,
        )

    def start(src, dst, sent, got, target):
        remote(src, dst, sent, got, target).start()

    def arrived(ref, got):
        remote(ref, ref, got, got, sib).wait_recv()

    def drained(ref, sent):
        remote(ref, ref, sent, sent, sib).wait_send()

    barrier = pltpu.get_barrier_semaphore()
    for peer in (zp, zm, yp, ym, yf, *xpeer.values(), sib):
        pl.semaphore_signal(barrier, inc=1, device_id=peer, device_id_type=MESH)

    own = buf.at[0, xs, c, y]
    half = KV // 2
    loads = [
        pltpu.make_async_copy(src, dst, s_loc.at[i])
        for i, (src, dst) in enumerate((
            (w_hbm, own),
            (d_hbm, dbuf.at[zl, xx]),
            (grads_hbm, raw),
            (up_hbm, up),
            (x_hbm, xv),
            (gain_hbm, gain),
        ))
    ]
    for cp in loads:
        cp.start()

    def pieces(s):
        return pl.ds(0, 1) if s == 0 else (pl.ds(15, 1) if s == 8 else pl.ds(2 * s - 1, 2))

    def z_slot(s, direction):
        return 0 if s == 0 else (15 if s == 8 else 2 * s - 1 + direction)

    def z_send(s, direction, kind, part):
        start(
            buf.at[z_slot(s - 1, direction), part, c, y],
            buf.at[z_slot(s, direction), part, c, y],
            z_, r_z.at[direction, s, kind], zm if direction else zp,
        )

    def z_step(s, kind):
        half_ = xs if kind == 0 else 1 - xs
        for direction in (0, 1):
            arrived(buf.at[z_slot(s, direction), half_, c, y], r_z.at[direction, s, kind])
            if s < 7:
                z_send(s + 1, direction, kind, half_)
            else:
                pl.when(half_ == direction)(functools.partial(far_copy(direction).start))

    def far_copy(direction):
        return remote(
            buf.at[z_slot(7, direction), direction, c, y], buf.at[15, direction, c, y],
            z_, r_z8.at[direction], zm if direction else zp,
        )

    def in_line(s, direction):
        return zl >= s if direction == 0 else zl + s < ZL

    def more(direction):
        return zl < ZL - 1 if direction == 0 else zl > 0

    def d_copy(s, direction, row):
        ref = dbuf.at[row, xx]
        sent = dz1 if direction else dz0
        return remote(ref, ref, sent, r_dz.at[direction, s], zm if direction else zp)

    def d_pair(s, direction):
        row = zl - s if direction == 0 else zl + s
        ok = in_line(s, direction) & (row % 2 == direction)
        return ok, row // 2

    def d_across(g):
        for d in (1, 2, 3):
            ref = dbuf.at[pl.ds(2 * g, 2), xx]
            start(ref, ref, d_, r_d.at[g], xpeer[d])

    def d_step(s):
        for direction in (0, 1):

            def go(direction=direction):
                row = zl - s if direction == 0 else zl + s
                arrived(dbuf.at[row, xx], r_dz.at[direction, s])

                def forward():
                    d_copy(s, direction, row).wait_send()
                    if s < 7:
                        d_copy(s + 1, direction, row).start()

                pl.when(more(direction))(forward)

            pl.when(in_line(s, direction))(go)
            pl.when((zl == (s - 1 if direction == 0 else 8 - s)) & more(direction))(
                lambda: d_copy(s, direction, zl).wait_send()
            )
            ok, g = d_pair(s, direction)
            pl.when(ok)(functools.partial(d_across, g))

    def d_done(s):
        for direction in (0, 1):
            ok, g = d_pair(s, direction)

            def go(g=g):
                arrived(dbuf.at[pl.ds(2 * g, 2), 0:3], r_d.at[g])

                def add(i, acc):
                    row = 2 * g + i // 4
                    return acc + dot(scaled[8 * g + i], dbuf[row, i % 4], NT)

                lin[...] += lax.fori_loop(0, 8, add, jnp.zeros((T, R), F32), unroll=8)

            pl.when(ok)(go)

    both = pl.ds(0, 2)
    direct_from = 8

    def y_send(s):
        src = buf.at[pieces(s), both, c, y]
        for peer in (yp, ym, yf) if s >= direct_from else (yp, ym):
            start(src, src, y1, r_y1.at[s], peer)

    def y_relay(s):
        arrived(buf.at[pieces(s), both, c, 0:2], r_y1.at[s])
        for direction, near, peer in ((0, y_down, yp), (1, y_up, ym)):
            src = buf.at[pieces(s), direction, c, near]
            start(src, src, y2, r_y2.at[s], peer)

    def y_done(s):
        if s >= direct_from:
            arrived(buf.at[pieces(s), both, c, 0:3], r_y1.at[s])
        else:
            arrived(buf.at[pieces(s), both, c, 0], r_y2.at[s])
        src = buf.at[pieces(s), both, c]
        start(src, src, sb, r_sib.at[s], sib)

    def sib_done(s):
        arrived(buf.at[pieces(s), both, 1 - c], r_sib.at[s])
        if s == 4:
            block(mod(zl + 4, ZL), 8, 7)
        elif s == 8:
            block(zl, 15, 0)
        elif s > 4:
            block(mod(zl + s, ZL), 2 * s, 15 - 2 * s)
            block(mod(zl - s, ZL), 2 * s - 1, 16 - 2 * s)

    def p_pairs(k):
        g = zl // 2
        if k == 4:
            return [(g >= 0, g)]
        return [(g + 4 - k < 4, g + 4 - k), (g - 4 + k >= 0, g - 4 + k)]

    def p_copy(d, g):
        return remote(
            part.at[mod(xx + d, NX), pl.ds(2 * g, 2)], part_in.at[d, pl.ds(2 * g, 2)],
            p_, r_p.at[g], xpeer[d],
        )

    def p_send(k):
        for ok, g in p_pairs(k):

            def go(g=g):
                def one(i, carry):
                    term = dot(lr_t, scaled[8 * g + i], NN)
                    part[i % 4, 2 * g + i // 4] = term.astype(BF16)
                    return carry

                lax.fori_loop(0, 8, one, 0, unroll=8)
                for d in (1, 2, 3):
                    p_copy(d, g).start()

            pl.when(ok)(go)

    def p_done(k):
        for ok, g in p_pairs(k):

            def go(g=g):
                arrived(part_in.at[1:4, pl.ds(2 * g, 2)], r_p.at[g])
                for i in (0, 1):
                    acc = part[xx, 2 * g + i].astype(F32)
                    for d in (1, 2, 3):
                        acc += part_in[d, 2 * g + i].astype(F32)
                    summed[2 * g + i] = acc

            pl.when(ok)(go)

    def c_copy(src, direction, j):
        return remote(
            src, chain.at[direction, j], c1 if direction else c0, r_c.at[direction, j],
            zm if direction else zp,
        )

    def c_step(j):
        for direction, place, row in ((0, zl, zl + 8 - j), (1, 7 - zl, zl - 8 + j)):

            def first(direction=direction, row=row):
                if j > 1:
                    c_copy(summed.at[0], direction, j - 1).wait_send()
                c_copy(summed.at[row], direction, j).start()

            pl.when(place == 0)(first)

            def later(direction=direction, place=place, row=row):
                here = chain.at[direction, j - 1]
                arrived(here, r_c.at[direction, j - 1])
                here[...] += summed[row]
                if j > 2:

                    @pl.when(place <= j - 2)
                    def _():
                        c_copy(here, direction, j - 1).wait_send()

                c_copy(here, direction, j).start()

            if j >= 2:
                pl.when((place >= 1) & (place <= j - 1))(later)

    def c_last():
        down[...] = summed[zl]
        for direction, place in ((0, zl), (1, 7 - zl)):

            def go(direction=direction):
                arrived(chain.at[direction, 7], r_c.at[direction, 7])
                down[...] += chain[direction, 7]

            pl.when(place >= 1)(go)
            pl.when(place <= 6)(
                functools.partial(c_copy(summed.at[0], direction, 7).wait_send)
            )
        pltpu.make_async_copy(down, down_out, s_loc.at[0]).start()

    def res_copy(n, row, p):
        tokens = pl.ds(64 * n, 64)
        return remote(
            res.at[row, :, pl.ds(T + 64 * n, 64)], fg.at[row, :, p, tokens], res_, r_res.at[row],
            xpeer[1 if n else 3],
        )

    def own_copy(row):
        return pltpu.make_async_copy(
            res.at[row, :, 0:T], fg.at[row, :, par], own_
        )

    def block(row, qa, qb):
        steps = (qa + 1) // 2
        first = (mod(z - steps, NZ) if qa % 2 else mod(z + steps, NZ)) // ZL

        def one(i, carry):
            acc = dot(tok[first], buf[qa, i].reshape(half, B), NN)
            acc += dot(tok[1 - first], buf[qb, i].reshape(half, B), NN)
            acc += dot(lr4[...], dbuf[row, par + 2 * i], NN)
            res[row, i] = acc.astype(BF16)
            return carry

        lax.fori_loop(0, 2, one, 0, unroll=2)
        for n in (0, 1):
            res_copy(n, row, par).start()
        own_copy(row).start()

    def core_major(values, h):
        blocks = [values[:, h * half + i * R:h * half + (i + 1) * R] for i in range(8)]
        return jnp.concatenate(blocks[0::2] + blocks[1::2], axis=1)

    def lowrank(rows):
        return (
            dot(tok[0, rows], up2[0], NT) + dot(tok[1, rows], up2[1], NT)
        ).astype(BF16)

    def pack_up():
        lb = lin[...].astype(BF16)
        for h in (0, 1):
            term = dot(tok[h, 0:T], lb, TN)
            term = term.reshape(2, NY, 2, 32, R).swapaxes(1, 2)
            upart[:, 4 * h:4 * h + 4] = term.reshape(NX, 4, 32, R).astype(BF16)
        for d in (1, 2, 3):
            start(upart.at[mod(xx + d, NX)], upart_in.at[d], u_, r_u, xpeer[d])

    def up_over_z():
        acc = upart[xx].astype(F32)
        arrived(upart_in.at[1:4], r_u)
        for d in (1, 2, 3):
            acc += upart_in[d].astype(F32)
        usum[...] = acc
        for d in (4, 3, 5, 2, 6, 1, 7):
            row = mod(zl + d, ZL)
            start(usum.at[row], uin.at[d], uz, r_uz, dev(zh * ZL + row, y, xx, c))

    def up_last():
        acc = usum[zl]
        arrived(uin.at[1:8], r_uz)
        for d in range(1, 8):
            acc += uin[d]
        upg[...] = acc
        pltpu.make_async_copy(upg, up_out, s_loc.at[1]).start()

    def square(i, acc):
        v = xv[:, pl.ds(pl.multiple_of(i * B, B), B)].astype(F32)
        return acc + v * v

    def make_scaled(i, carry):
        columns = pl.ds(pl.multiple_of(i * B, B), B)
        scaled[i] = (xv[:, columns].astype(F32) * inv[...] * gain[:, columns]).astype(BF16)
        return carry

    for i in (0, 1):
        loads[i].wait()
    pl.semaphore_wait(barrier, 9)

    start(own, own, w2, r_w2, xpeer[2])
    for direction in (0, 1):
        z_send(1, direction, 0, xs)
    for direction in (0, 1):
        pl.when(more(direction))(functools.partial(d_copy(1, direction, zl).start))
    loads[2].wait()
    for h in (0, 1):
        tok[h, 0:T] = core_major(raw[...], h)
    for n in (0, 1):
        start(
            tok.at[:, 64 * n:64 * n + 64], tok.at[:, T + 64 * n:T + 64 * n + 64],
            g_, r_g, xpeer[3 if n else 1],
        )
    loads[4].wait()
    total = lax.fori_loop(0, 32, square, jnp.zeros((T, B), F32), unroll=2)
    inv[...] = lax.rsqrt(jnp.sum(total, axis=1, keepdims=True) / D + norm_eps)

    arrived(buf.at[0, 1 - xs, c, y], r_w2)
    for direction in (0, 1):
        z_send(1, direction, 1, 1 - xs)
    y_send(0)

    loads[3].wait()
    for h in (0, 1):
        up2[h] = core_major(up[...], h)
    lr_t = (dot(up2[0], tok[0, 0:T], NT) + dot(up2[1], tok[1, 0:T], NT)).astype(BF16)
    lr4[0:T] = lowrank(slice(0, T)) * adapter_scale
    lin[...] = jnp.zeros_like(lin)
    loads[5].wait()
    lax.fori_loop(0, 32, make_scaled, 0, unroll=2)
    p_send(1)

    d_at = {1: (1,), 2: (2,), 3: (3,), 4: (4,), 5: (5, 6), 6: (7,)}
    d_done_at = {3: (1,), 4: (2,), 5: (3,), 6: (4, 5), 7: (6, 7)}
    for s in range(1, 9):
        if s <= 7:
            z_step(s, 0)
            z_step(s, 1)
        else:
            for direction in (0, 1):
                arrived(buf.at[15, direction, c, y], r_z8.at[direction])
        y_send(s)
        for v in d_at.get(s, ()):
            d_step(v)
        y_relay(s - 1)
        if s >= 2:
            y_done(s - 2)
        if s >= 3:
            sib_done(s - 3)
        if s == 1:
            arrived(tok.at[:, T:2 * T], r_g)
            lr4[T:] = lowrank(slice(T, 2 * T)) * adapter_scale
        if s in (1, 3, 5):
            p_send((s + 3) // 2)
        if s % 2 == 0 and s < 8:
            p_done(s // 2)
        if 2 <= s < 8:
            c_step(s - 1)
        for v in d_done_at.get(s, ()):
            d_done(v)
        if s == 7:
            pack_up()

    y_done(7)
    y_done(8)
    up_over_z()
    sib_done(6)
    p_done(4)
    c_step(7)
    sib_done(7)
    sib_done(8)
    c_last()
    up_last()
    with jax.named_scope("features_wait"):
        for row in range(ZL):
            arrived(fg.at[row, :, 1 - par], r_res.at[row])
    with jax.named_scope("sends_wait"):
        drained(own, w2)
        drained(tok.at[:, 0:T], g_)
        drained(buf.at[0:15, 0, 0, 0:2], z_)
        drained(buf.at[0:11, 0:2, 0, 0:3], y1)
        drained(buf.at[0:15, 0, 0, 0:2], y2)
        drained(buf.at[0:16, 0:2, 0], sb)
        drained(dbuf.at[:, 0:3], d_)
        drained(part.at[0:3], p_)
        drained(res.at[:, 0:1], res_)
        drained(upart.at[1:4], u_)
        drained(usum.at[1:8], uz)
        pltpu.make_async_copy(res.at[:, :, 0:T], fg.at[:, :, par], own_).wait()
        pltpu.make_async_copy(down, down_out, s_loc.at[0]).wait()
        pltpu.make_async_copy(upg, up_out, s_loc.at[1]).wait()


def exchange(x, grads, w, d, up, gain):
    sem = pltpu.SemaphoreType.DMA
    hbm = pl.BlockSpec(memory_space=pl.ANY)
    return pl.pallas_call(
        main_kernel,
        out_shape=(
            jax.ShapeDtypeStruct((ZL, 2, 2, T, B), BF16),
            jax.ShapeDtypeStruct((R, B), F32),
            jax.ShapeDtypeStruct((32, R), F32),
        ),
        in_specs=[hbm] * 6,
        out_specs=(hbm, hbm, hbm),
        scratch_shapes=[
            pltpu.VMEM((T, D), BF16),
            pltpu.VMEM((T, KV), BF16),
            pltpu.VMEM((R, KV), BF16),
            pltpu.VMEM((2, R, KV // 2), BF16),
            pltpu.VMEM((1, D), F32),
            pltpu.VMEM((32, T, B), BF16),
            pltpu.VMEM((16, 2, 2, NY, R, B), BF16),
            pltpu.VMEM((ZL, NX, R, B), BF16),
            pltpu.VMEM((2, 2 * T, KV // 2), BF16),
            pltpu.VMEM((2 * T, R), BF16),
            pltpu.VMEM((ZL, 2, 2 * T, B), BF16),
            pltpu.VMEM((T, 1), F32),
            pltpu.VMEM((NX, ZL, R, B), BF16),
            pltpu.VMEM((NX, ZL, R, B), BF16),
            pltpu.VMEM((ZL, R, B), F32),
            pltpu.VMEM((2, 8, R, B), F32),
            pltpu.VMEM((T, R), F32),
            pltpu.VMEM((NX, ZL, 32, R), BF16),
            pltpu.VMEM((NX, ZL, 32, R), BF16),
            pltpu.VMEM((ZL, 32, R), F32),
            pltpu.VMEM((ZL, 32, R), F32),
            pltpu.VMEM((R, B), F32),
            pltpu.VMEM((32, R), F32),
            sem((6,)),
            sem((16,)),
            sem((4,)),
            sem((2, 8, 2)),
            sem((2,)),
            sem((2, 8)),
            sem((9,)),
            sem((9,)),
            sem((9,)),
            sem((4,)),
            sem((4,)),
            sem((2, 8)),
            sem((8,)),
        ],
        compiler_params=pltpu.CompilerParams(
            collective_id=1, has_side_effects=True, vmem_limit_bytes=60 << 20
        ),
        name="exchange",
    )(x, grads, w, d, up, gain)


def finish_kernel(scaling, x, fg, gain, down, up, out, down_out, up_out):
    @pl.when(pl.program_id(0) == 0)
    def _():
        down_out[...] = scaling * down[...]
        up_out[...] = scaling * up[...]

    rows = x.shape[0]
    squares = jnp.zeros((rows, B), F32)
    products = jnp.zeros((rows, B), F32)
    for i in range(32):
        v = x[:, i * B:(i + 1) * B].astype(F32)
        g = fg[i // 4, (i % 4) // 2, i % 2].astype(F32) * gain[:, i * B:(i + 1) * B]
        squares += v * v
        products += v * g
    inv = lax.rsqrt(jnp.sum(squares, axis=1, keepdims=True) / D + norm_eps)
    slope = inv * inv * (jnp.sum(products, axis=1, keepdims=True) / D)
    for i in range(32):
        v = x[:, i * B:(i + 1) * B].astype(F32)
        g = fg[i // 4, (i % 4) // 2, i % 2].astype(F32) * gain[:, i * B:(i + 1) * B]
        out[:, i * B:(i + 1) * B] = (inv * (g - v * slope)).astype(BF16)


def finish(x, fg, gain, down, up, scaling):
    rows = 64

    def whole(*shape):
        return pl.BlockSpec(shape, lambda i: (0,) * len(shape))

    return pl.pallas_call(
        functools.partial(finish_kernel, scaling),
        grid=(T // rows,),
        out_shape=(
            jax.ShapeDtypeStruct((T, D), BF16),
            jax.ShapeDtypeStruct((R, B), F32),
            jax.ShapeDtypeStruct((32, R), F32),
        ),
        in_specs=[
            pl.BlockSpec((rows, D), lambda i: (i, 0)),
            pl.BlockSpec((ZL, 2, 2, rows, B), lambda i: (0, 0, 0, i, 0)),
            whole(1, D), whole(R, B), whole(32, R),
        ],
        out_specs=(pl.BlockSpec((rows, D), lambda i: (i, 0)), whole(R, B), whole(32, R)),
        compiler_params=pltpu.CompilerParams(vmem_limit_bytes=60 << 20),
        name="finish",
    )(x, fg, gain, down, up)


def per_device(layer_input, value_grads, value_weight, adapter_down, adapter_up, norm_gain):
    scaling = gradient_scale / math.sqrt(layer_input.shape[1] * lax.axis_size("tensor"))
    gain = norm_gain.reshape(1, D)
    fg, down_t, up_t = exchange(
        layer_input[0], value_grads[0], value_weight.T, adapter_down[0].T, adapter_up[0], gain
    )
    input_grads, down_grads, up_grads = finish(
        layer_input[0], fg, gain, down_t, up_t, scaling
    )
    return (input_grads[None], down_grads.T[None], up_grads.T[None])


def solution(mesh):
    return jax.shard_map(
        per_device,
        mesh=mesh,
        in_specs=(
            P("member", "tensor", None),
            P("member", "tensor", None),
            P("tensor", "member"),
            P("member", "tensor", None),
            P("member", None, None),
            P(),
        ),
        out_specs=(
            P("member", "tensor", None),
            P("member", "tensor", None),
            P("member", None, "tensor"),
        ),
        check_vma=False,
    )
```

```python
import functools
import math

import jax
import jax.numpy as jnp
from jax import lax
from jax.experimental import pallas as pl
from jax.experimental.pallas import tpu as pltpu
from jax.sharding import PartitionSpec as P

adapter_scale = 4.0
gradient_scale = 1.0
norm_eps = 1e-05

F32 = jnp.float32
BF16 = jnp.bfloat16
MESH = pl.DeviceIdType.MESH
ZL, ZH, NX, NY = 8, 2, 4, 4
NZ = ZL * ZH
D = 8192
KV = 1024
R = 64
T = 128
B = 256
NN = (((1,), (0,)), ((), ()))
NT = (((1,), (1,)), ((), ()))
TN = (((0,), (0,)), ((), ()))


def dot(a, b, dims):
    return lax.dot_general(a, b, dims, preferred_element_type=F32)


def mod(a, n):
    return lax.rem(a + 4 * n, n)


def main_kernel(
    x_hbm, grads_hbm, w_hbm, d_hbm, up_hbm, gain_hbm,
    fg, down_out, up_out,
    xv, raw, up, up2, gain, scaled, buf, dbuf, tok, lr4, res, inv,
    part, part_in, summed, chain, lin, upart, upart_in, usum, uin,
    down, upg, s_loc, s_send, r_yz, r_one, r_z, r_z8, r_dz, r_y1, r_y2, r_sib, r_d, r_p, r_c, r_res,
):
    m = lax.axis_index("member")
    t = lax.axis_index("tensor")
    zh, y, c = m // 8, (m // 2) % 4, m % 2
    zl, xx = t // 4, t % 4
    z = zh * ZL + zl
    par, xs = xx % 2, xx // 2

    def dev(z_, y_, x_, c_):
        return ((z_ // ZL) * 8 + y_ * 2 + c_, (z_ % ZL) * 4 + x_)

    y_up, y_down, y_far = mod(y + 1, NY), mod(y - 1, NY), mod(y + 2, NY)
    zp, zm = dev(mod(z + 1, NZ), y, xx, c), dev(mod(z - 1, NZ), y, xx, c)
    yp, ym, yf = dev(z, y_up, xx, c), dev(z, y_down, xx, c), dev(z, y_far, xx, c)
    sib = dev(z, y, xx, 1 - c)
    xpeer = {d: dev(z, y, mod(xx + d, NX), c) for d in (1, 2, 3)}

    (w2, g_, z_, y1, y2, yz, sb, d_, p_, res_, u_, uz, own_, dz0, dz1, c0, c1) = [
        s_send.at[i] for i in range(17)
    ]
    r_w2, r_g, r_u, r_uz = [r_one.at[i] for i in range(4)]

    def remote(src, dst, sent, got, target):
        return pltpu.make_async_remote_copy(
            src_ref=src, dst_ref=dst, send_sem=sent, recv_sem=got,
            device_id=target, device_id_type=MESH,
        )

    def start(src, dst, sent, got, target):
        remote(src, dst, sent, got, target).start()

    def arrived(ref, got):
        remote(ref, ref, got, got, sib).wait_recv()

    def drained(ref, sent):
        remote(ref, ref, sent, sent, sib).wait_send()

    barrier = pltpu.get_barrier_semaphore()
    for peer in (zp, zm, yp, ym, *xpeer.values(), sib):
        pl.semaphore_signal(barrier, inc=1, device_id=peer, device_id_type=MESH)

    own = buf.at[0, xs, c, y]
    half = KV // 2
    loads = [
        pltpu.make_async_copy(src, dst, s_loc.at[i])
        for i, (src, dst) in enumerate((
            (w_hbm, own),
            (d_hbm, dbuf.at[zl, xx]),
            (grads_hbm, raw),
            (up_hbm, up),
            (x_hbm, xv),
            (gain_hbm, gain),
        ))
    ]
    for cp in loads:
        cp.start()

    def pieces(s):
        return pl.ds(0, 1) if s == 0 else (pl.ds(15, 1) if s == 8 else pl.ds(2 * s - 1, 2))

    def z_slot(s, direction):
        return 0 if s == 0 else (15 if s == 8 else 2 * s - 1 + direction)

    def z_send(s, direction, kind, part):
        start(
            buf.at[z_slot(s - 1, direction), part, c, y],
            buf.at[z_slot(s, direction), part, c, y],
            z_, r_z.at[direction, s, kind], zm if direction else zp,
        )

    def z_step(s, kind):
        half_ = xs if kind == 0 else 1 - xs
        for direction in (0, 1):
            arrived(buf.at[z_slot(s, direction), half_, c, y], r_z.at[direction, s, kind])
            if s < 7:
                z_send(s + 1, direction, kind, half_)
            else:
                pl.when(half_ == direction)(functools.partial(far_copy(direction).start))

    def far_copy(direction):
        return remote(
            buf.at[z_slot(7, direction), direction, c, y], buf.at[15, direction, c, y],
            z_, r_z8.at[direction], zm if direction else zp,
        )

    def in_line(s, direction):
        return zl >= s if direction == 0 else zl + s < ZL

    def more(direction):
        return zl < ZL - 1 if direction == 0 else zl > 0

    def d_copy(s, direction, row):
        ref = dbuf.at[row, xx]
        sent = dz1 if direction else dz0
        return remote(ref, ref, sent, r_dz.at[direction, s], zm if direction else zp)

    def d_pair(s, direction):
        row = zl - s if direction == 0 else zl + s
        ok = in_line(s, direction) & (row % 2 == direction)
        return ok, row // 2

    def d_across(g):
        for d in (1, 2, 3):
            ref = dbuf.at[pl.ds(2 * g, 2), xx]
            start(ref, ref, d_, r_d.at[g], xpeer[d])

    def d_step(s):
        for direction in (0, 1):

            def go(direction=direction):
                row = zl - s if direction == 0 else zl + s
                arrived(dbuf.at[row, xx], r_dz.at[direction, s])

                def forward():
                    d_copy(s, direction, row).wait_send()
                    if s < 7:
                        d_copy(s + 1, direction, row).start()

                pl.when(more(direction))(forward)

            pl.when(in_line(s, direction))(go)
            pl.when((zl == (s - 1 if direction == 0 else 8 - s)) & more(direction))(
                lambda: d_copy(s, direction, zl).wait_send()
            )
            ok, g = d_pair(s, direction)
            pl.when(ok)(functools.partial(d_across, g))

    def d_done(s):
        for direction in (0, 1):
            ok, g = d_pair(s, direction)

            def go(g=g):
                arrived(dbuf.at[pl.ds(2 * g, 2), 0:3], r_d.at[g])

                def add(i, acc):
                    row = 2 * g + i // 4
                    return acc + dot(scaled[8 * g + i], dbuf[row, i % 4], NT)

                lin[...] += lax.fori_loop(0, 8, add, jnp.zeros((T, R), F32), unroll=8)

            pl.when(ok)(go)

    both = pl.ds(0, 2)
    halves = (xs, 1 - xs)

    def y_send(s, kind):
        src = buf.at[pieces(s), halves[kind], c, y]
        for peer in (yp, ym):
            start(src, src, y1, r_y1.at[s, kind], peer)

    def y_send_far():
        src = buf.at[pieces(8), both, c, y]
        for peer in (yp, ym, yf):
            start(src, src, y2, r_y1.at[8, 0], peer)

    def z_whole(k):
        other = mod(y + k, NY)
        for direction, peer in ((0, zp), (1, zm)):
            start(
                buf.at[0, both, c, other], buf.at[1 + direction, both, c, other],
                yz, r_yz.at[direction], peer,
            )

    def y_relay(s, kind):
        half_ = halves[kind]
        arrived(buf.at[pieces(s), half_, c, 0:2], r_y1.at[s, kind])
        src = buf.at[pieces(s), half_, c, mod(y - 1 + 2 * half_, NY)]
        start(src, src, y2, r_y2.at[s], dev(z, mod(y + 1 - 2 * half_, NY), xx, c))

    def y_done(s):
        if s == 8:
            arrived(buf.at[pieces(s), both, c, 0:3], r_y1.at[s, 0])
        elif s == 1:
            for direction in (0, 1):
                arrived(buf.at[1 + direction, both, c, 0:3], r_yz.at[direction])
        else:
            arrived(buf.at[pieces(s), both, c, 0], r_y2.at[s])
        src = buf.at[pieces(s), both, c]
        start(src, src, sb, r_sib.at[s], sib)

    def sib_done(s):
        arrived(buf.at[pieces(s), both, 1 - c], r_sib.at[s])
        if s == 4:
            block(mod(zl + 4, ZL), 8, 7)
        elif s == 8:
            block(zl, 15, 0)
        elif s > 4:
            block(mod(zl + s, ZL), 2 * s, 15 - 2 * s)
            block(mod(zl - s, ZL), 2 * s - 1, 16 - 2 * s)

    def p_pairs(k):
        g = zl // 2
        if k == 4:
            return [(g >= 0, g)]
        return [(g + 4 - k < 4, g + 4 - k), (g - 4 + k >= 0, g - 4 + k)]

    def p_copy(d, g):
        return remote(
            part.at[mod(xx + d, NX), pl.ds(2 * g, 2)], part_in.at[d, pl.ds(2 * g, 2)],
            p_, r_p.at[g], xpeer[d],
        )

    def p_send(k):
        for ok, g in p_pairs(k):

            def go(g=g):
                def one(i, carry):
                    term = dot(lr_t, scaled[8 * g + i], NN)
                    part[i % 4, 2 * g + i // 4] = term.astype(BF16)
                    return carry

                lax.fori_loop(0, 8, one, 0, unroll=8)
                for d in (1, 2, 3):
                    p_copy(d, g).start()

            pl.when(ok)(go)

    def p_done(k):
        for ok, g in p_pairs(k):

            def go(g=g):
                arrived(part_in.at[1:4, pl.ds(2 * g, 2)], r_p.at[g])
                for i in (0, 1):
                    acc = part[xx, 2 * g + i].astype(F32)
                    for d in (1, 2, 3):
                        acc += part_in[d, 2 * g + i].astype(F32)
                    summed[2 * g + i] = acc

            pl.when(ok)(go)

    def c_copy(src, direction, j):
        return remote(
            src, chain.at[direction, j], c1 if direction else c0, r_c.at[direction, j],
            zm if direction else zp,
        )

    def c_step(j):
        for direction, place, row in ((0, zl, zl + 8 - j), (1, 7 - zl, zl - 8 + j)):

            def first(direction=direction, row=row):
                if j > 1:
                    c_copy(summed.at[0], direction, j - 1).wait_send()
                c_copy(summed.at[row], direction, j).start()

            pl.when(place == 0)(first)

            def later(direction=direction, place=place, row=row):
                here = chain.at[direction, j - 1]
                arrived(here, r_c.at[direction, j - 1])
                here[...] += summed[row]
                if j > 2:

                    @pl.when(place <= j - 2)
                    def _():
                        c_copy(here, direction, j - 1).wait_send()

                c_copy(here, direction, j).start()

            if j >= 2:
                pl.when((place >= 1) & (place <= j - 1))(later)

    def c_last():
        down[...] = summed[zl]
        for direction, place in ((0, zl), (1, 7 - zl)):

            def go(direction=direction):
                arrived(chain.at[direction, 7], r_c.at[direction, 7])
                down[...] += chain[direction, 7]

            pl.when(place >= 1)(go)
            pl.when(place <= 6)(
                functools.partial(c_copy(summed.at[0], direction, 7).wait_send)
            )
        pltpu.make_async_copy(down, down_out, s_loc.at[0]).start()

    def res_copy(n, row, p):
        tokens = pl.ds(64 * n, 64)
        return remote(
            res.at[row, :, pl.ds(T + 64 * n, 64)], fg.at[row, :, p, tokens], res_, r_res.at[row],
            xpeer[1 if n else 3],
        )

    def own_copy(row):
        return pltpu.make_async_copy(
            res.at[row, :, 0:T], fg.at[row, :, par], own_
        )

    def block(row, qa, qb):
        steps = (qa + 1) // 2
        first = (mod(z - steps, NZ) if qa % 2 else mod(z + steps, NZ)) // ZL

        def one(i, carry):
            acc = dot(tok[first], buf[qa, i].reshape(half, B), NN)
            acc += dot(tok[1 - first], buf[qb, i].reshape(half, B), NN)
            acc += dot(lr4[...], dbuf[row, par + 2 * i], NN)
            res[row, i] = acc.astype(BF16)
            return carry

        lax.fori_loop(0, 2, one, 0, unroll=2)
        for n in (0, 1):
            res_copy(n, row, par).start()
        own_copy(row).start()

    def core_major(values, h):
        blocks = [values[:, h * half + i * R:h * half + (i + 1) * R] for i in range(8)]
        return jnp.concatenate(blocks[0::2] + blocks[1::2], axis=1)

    def lowrank(rows):
        return (
            dot(tok[0, rows], up2[0], NT) + dot(tok[1, rows], up2[1], NT)
        ).astype(BF16)

    def pack_up():
        lb = lin[...].astype(BF16)
        for h in (0, 1):
            term = dot(tok[h, 0:T], lb, TN)
            term = term.reshape(2, NY, 2, 32, R).swapaxes(1, 2)
            upart[:, 4 * h:4 * h + 4] = term.reshape(NX, 4, 32, R).astype(BF16)
        for d in (1, 2, 3):
            start(upart.at[mod(xx + d, NX)], upart_in.at[d], u_, r_u, xpeer[d])

    def up_over_z():
        acc = upart[xx].astype(F32)
        arrived(upart_in.at[1:4], r_u)
        for d in (1, 2, 3):
            acc += upart_in[d].astype(F32)
        usum[...] = acc
        for d in (4, 3, 5, 2, 6, 1, 7):
            row = mod(zl + d, ZL)
            start(usum.at[row], uin.at[d], uz, r_uz, dev(zh * ZL + row, y, xx, c))

    def up_last():
        acc = usum[zl]
        arrived(uin.at[1:8], r_uz)
        for d in range(1, 8):
            acc += uin[d]
        upg[...] = acc
        pltpu.make_async_copy(upg, up_out, s_loc.at[1]).start()

    def square(i, acc):
        v = xv[:, pl.ds(pl.multiple_of(i * B, B), B)].astype(F32)
        return acc + v * v

    def make_scaled(i, carry):
        columns = pl.ds(pl.multiple_of(i * B, B), B)
        scaled[i] = (xv[:, columns].astype(F32) * inv[...] * gain[:, columns]).astype(BF16)
        return carry

    for i in (0, 1):
        loads[i].wait()
    pl.semaphore_wait(barrier, 8)

    start(own, own, w2, r_w2, xpeer[2])
    for direction in (0, 1):
        z_send(1, direction, 0, xs)
    y_send(0, 0)
    for direction in (0, 1):
        pl.when(more(direction))(functools.partial(d_copy(1, direction, zl).start))
    loads[2].wait()
    for h in (0, 1):
        tok[h, 0:T] = core_major(raw[...], h)
    for n in (0, 1):
        start(
            tok.at[:, 64 * n:64 * n + 64], tok.at[:, T + 64 * n:T + 64 * n + 64],
            g_, r_g, xpeer[3 if n else 1],
        )
    loads[4].wait()
    total = lax.fori_loop(0, 32, square, jnp.zeros((T, B), F32), unroll=2)
    inv[...] = lax.rsqrt(jnp.sum(total, axis=1, keepdims=True) / D + norm_eps)

    arrived(buf.at[0, 1 - xs, c, y], r_w2)
    for direction in (0, 1):
        z_send(1, direction, 1, 1 - xs)
    y_send(0, 1)

    loads[3].wait()
    for h in (0, 1):
        up2[h] = core_major(up[...], h)
    lr_t = (dot(up2[0], tok[0, 0:T], NT) + dot(up2[1], tok[1, 0:T], NT)).astype(BF16)
    lr4[0:T] = lowrank(slice(0, T)) * adapter_scale
    lin[...] = jnp.zeros_like(lin)
    loads[5].wait()
    lax.fori_loop(0, 32, make_scaled, 0, unroll=2)
    p_send(1)

    d_done_at = {3: (1,), 4: (2,), 5: (3,), 6: (4,), 7: (5,)}
    p_done_at = {3: 1, 5: 2, 7: 3}
    y_done_at = {2: (0,), 5: (1, 2), 6: (3, 4), 7: (5,)}
    for s in range(1, 8):
        for kind in (0, 1):
            z_step(s, kind)
            if s > 1:
                y_send(s, kind)
        if s != 2:
            y_relay(s - 1, 0)
            y_relay(s - 1, 1)
        if s <= 6:
            d_step(s)
        for v in y_done_at.get(s, ()):
            y_done(v)
        if 2 <= s <= 4:
            z_whole(s - 1)
        if s == 1:
            arrived(tok.at[:, T:2 * T], r_g)
            lr4[T:] = lowrank(slice(T, 2 * T)) * adapter_scale
        if s in (1, 3, 5):
            p_send((s + 3) // 2)
        if s in p_done_at:
            p_done(p_done_at[s])
        if s >= 3:
            c_step(s - 2)
        for v in d_done_at.get(s, ()):
            d_done(v)
        if s == 6:
            d_step(7)

    y_relay(7, 0)
    y_relay(7, 1)
    for direction in (0, 1):
        arrived(buf.at[15, direction, c, y], r_z8.at[direction])
    y_send_far()
    y_done(6)
    c_step(6)
    p_done(4)
    d_done(6)
    d_done(7)
    pack_up()
    sib_done(4)
    sib_done(3)
    sib_done(5)
    y_done(7)
    y_done(8)
    up_over_z()
    sib_done(2)
    sib_done(6)
    c_step(7)
    sib_done(1)
    sib_done(7)
    sib_done(0)
    sib_done(8)
    c_last()
    up_last()
    with jax.named_scope("features_wait"):
        for row in range(ZL):
            arrived(fg.at[row, :, 1 - par], r_res.at[row])
    with jax.named_scope("sends_wait"):
        drained(own, w2)
        drained(tok.at[:, 0:T], g_)
        drained(buf.at[0:15, 0, 0, 0:2], z_)
        drained(buf.at[0:13, 0, 0], y1)
        drained(buf.at[0:16, 0, 0, 0:2], y2)
        drained(buf.at[0:3, 0, 0], yz)
        drained(buf.at[0:16, 0:2, 0], sb)
        drained(dbuf.at[:, 0:3], d_)
        drained(part.at[0:3], p_)
        drained(res.at[:, 0:1], res_)
        drained(upart.at[1:4], u_)
        drained(usum.at[1:8], uz)
        pltpu.make_async_copy(res.at[:, :, 0:T], fg.at[:, :, par], own_).wait()
        pltpu.make_async_copy(down, down_out, s_loc.at[0]).wait()
        pltpu.make_async_copy(upg, up_out, s_loc.at[1]).wait()


def exchange(x, grads, w, d, up, gain):
    sem = pltpu.SemaphoreType.DMA
    hbm = pl.BlockSpec(memory_space=pl.ANY)
    return pl.pallas_call(
        main_kernel,
        out_shape=(
            jax.ShapeDtypeStruct((ZL, 2, 2, T, B), BF16),
            jax.ShapeDtypeStruct((R, B), F32),
            jax.ShapeDtypeStruct((32, R), F32),
        ),
        in_specs=[hbm] * 6,
        out_specs=(hbm, hbm, hbm),
        scratch_shapes=[
            pltpu.VMEM((T, D), BF16),
            pltpu.VMEM((T, KV), BF16),
            pltpu.VMEM((R, KV), BF16),
            pltpu.VMEM((2, R, KV // 2), BF16),
            pltpu.VMEM((1, D), F32),
            pltpu.VMEM((32, T, B), BF16),
            pltpu.VMEM((16, 2, 2, NY, R, B), BF16),
            pltpu.VMEM((ZL, NX, R, B), BF16),
            pltpu.VMEM((2, 2 * T, KV // 2), BF16),
            pltpu.VMEM((2 * T, R), BF16),
            pltpu.VMEM((ZL, 2, 2 * T, B), BF16),
            pltpu.VMEM((T, 1), F32),
            pltpu.VMEM((NX, ZL, R, B), BF16),
            pltpu.VMEM((NX, ZL, R, B), BF16),
            pltpu.VMEM((ZL, R, B), F32),
            pltpu.VMEM((2, 8, R, B), F32),
            pltpu.VMEM((T, R), F32),
            pltpu.VMEM((NX, ZL, 32, R), BF16),
            pltpu.VMEM((NX, ZL, 32, R), BF16),
            pltpu.VMEM((ZL, 32, R), F32),
            pltpu.VMEM((ZL, 32, R), F32),
            pltpu.VMEM((R, B), F32),
            pltpu.VMEM((32, R), F32),
            sem((6,)),
            sem((17,)),
            sem((2,)),
            sem((4,)),
            sem((2, 8, 2)),
            sem((2,)),
            sem((2, 8)),
            sem((9, 2)),
            sem((9,)),
            sem((9,)),
            sem((4,)),
            sem((4,)),
            sem((2, 8)),
            sem((8,)),
        ],
        compiler_params=pltpu.CompilerParams(
            collective_id=1, has_side_effects=True, vmem_limit_bytes=60 << 20
        ),
        name="exchange",
    )(x, grads, w, d, up, gain)


def finish_kernel(scaling, x, fg, gain, down, up, out, down_out, up_out):
    @pl.when(pl.program_id(0) == 0)
    def _():
        down_out[...] = scaling * down[...]
        up_out[...] = scaling * up[...]

    rows = x.shape[0]
    squares = jnp.zeros((rows, B), F32)
    products = jnp.zeros((rows, B), F32)
    for i in range(32):
        v = x[:, i * B:(i + 1) * B].astype(F32)
        g = fg[i // 4, (i % 4) // 2, i % 2].astype(F32) * gain[:, i * B:(i + 1) * B]
        squares += v * v
        products += v * g
    inv = lax.rsqrt(jnp.sum(squares, axis=1, keepdims=True) / D + norm_eps)
    slope = inv * inv * (jnp.sum(products, axis=1, keepdims=True) / D)
    for i in range(32):
        v = x[:, i * B:(i + 1) * B].astype(F32)
        g = fg[i // 4, (i % 4) // 2, i % 2].astype(F32) * gain[:, i * B:(i + 1) * B]
        out[:, i * B:(i + 1) * B] = (inv * (g - v * slope)).astype(BF16)


def finish(x, fg, gain, down, up, scaling):
    rows = 64

    def whole(*shape):
        return pl.BlockSpec(shape, lambda i: (0,) * len(shape))

    return pl.pallas_call(
        functools.partial(finish_kernel, scaling),
        grid=(T // rows,),
        out_shape=(
            jax.ShapeDtypeStruct((T, D), BF16),
            jax.ShapeDtypeStruct((R, B), F32),
            jax.ShapeDtypeStruct((32, R), F32),
        ),
        in_specs=[
            pl.BlockSpec((rows, D), lambda i: (i, 0)),
            pl.BlockSpec((ZL, 2, 2, rows, B), lambda i: (0, 0, 0, i, 0)),
            whole(1, D), whole(R, B), whole(32, R),
        ],
        out_specs=(pl.BlockSpec((rows, D), lambda i: (i, 0)), whole(R, B), whole(32, R)),
        compiler_params=pltpu.CompilerParams(vmem_limit_bytes=60 << 20),
        name="finish",
    )(x, fg, gain, down, up)


def per_device(layer_input, value_grads, value_weight, adapter_down, adapter_up, norm_gain):
    scaling = gradient_scale / math.sqrt(layer_input.shape[1] * lax.axis_size("tensor"))
    gain = norm_gain.reshape(1, D)
    fg, down_t, up_t = exchange(
        layer_input[0], value_grads[0], value_weight.T, adapter_down[0].T, adapter_up[0], gain
    )
    input_grads, down_grads, up_grads = finish(
        layer_input[0], fg, gain, down_t, up_t, scaling
    )
    return (input_grads[None], down_grads.T[None], up_grads.T[None])


def solution(mesh):
    return jax.shard_map(
        per_device,
        mesh=mesh,
        in_specs=(
            P("member", "tensor", None),
            P("member", "tensor", None),
            P("tensor", "member"),
            P("member", "tensor", None),
            P("member", None, None),
            P(),
        ),
        out_specs=(
            P("member", "tensor", None),
            P("member", "tensor", None),
            P("member", None, "tensor"),
        ),
        check_vma=False,
    )
```

```python
import functools
import math

import jax
import jax.numpy as jnp
from jax import lax
from jax.experimental import pallas as pl
from jax.experimental.pallas import tpu as pltpu
from jax.sharding import PartitionSpec as P

adapter_scale = 4.0
gradient_scale = 1.0
norm_eps = 1e-05

F32 = jnp.float32
BF16 = jnp.bfloat16
MESH = pl.DeviceIdType.MESH
ZL, ZH, NX, NY = 8, 2, 4, 4
NZ = ZL * ZH
D = 8192
KV = 1024
R = 64
T = 128
B = 256
NN = (((1,), (0,)), ((), ()))
NT = (((1,), (1,)), ((), ()))
TN = (((0,), (0,)), ((), ()))


def dot(a, b, dims):
    return lax.dot_general(a, b, dims, preferred_element_type=F32)


def mod(a, n):
    return lax.rem(a + 4 * n, n)


def main_kernel(
    x_hbm, grads_hbm, w_hbm, d_hbm, up_hbm, gain_hbm,
    fg, down_out, up_out,
    xv, raw, up, up2, gain, scaled, buf, dbuf, tok, lr4, res, inv,
    part, part_in, summed, chain, lin, upart, upart_in, usum, uin,
    down, upg, s_loc, s_send, r_yz, r_one, r_z, r_z8, r_dz, r_y1, r_y2, r_sib, r_d, r_p, r_c, r_res,
):
    m = lax.axis_index("member")
    t = lax.axis_index("tensor")
    zh, y, c = m // 8, (m // 2) % 4, m % 2
    zl, xx = t // 4, t % 4
    z = zh * ZL + zl
    par, xs = xx % 2, xx // 2

    def dev(z_, y_, x_, c_):
        return ((z_ // ZL) * 8 + y_ * 2 + c_, (z_ % ZL) * 4 + x_)

    y_up, y_down, y_far = mod(y + 1, NY), mod(y - 1, NY), mod(y + 2, NY)
    zp, zm = dev(mod(z + 1, NZ), y, xx, c), dev(mod(z - 1, NZ), y, xx, c)
    yp, ym, yf = dev(z, y_up, xx, c), dev(z, y_down, xx, c), dev(z, y_far, xx, c)
    sib = dev(z, y, xx, 1 - c)
    xpeer = {d: dev(z, y, mod(xx + d, NX), c) for d in (1, 2, 3)}

    (w2, g_, z_, y1, y2, yz, sb, d_, p_, res_, u_, uz, own_, dz0, dz1, c0, c1) = [
        s_send.at[i] for i in range(17)
    ]
    r_w2, r_g, r_u, r_uz = [r_one.at[i] for i in range(4)]

    def remote(src, dst, sent, got, target):
        return pltpu.make_async_remote_copy(
            src_ref=src, dst_ref=dst, send_sem=sent, recv_sem=got,
            device_id=target, device_id_type=MESH,
        )

    def start(src, dst, sent, got, target):
        remote(src, dst, sent, got, target).start()

    def arrived(ref, got):
        remote(ref, ref, got, got, sib).wait_recv()

    def drained(ref, sent):
        remote(ref, ref, sent, sent, sib).wait_send()

    barrier = pltpu.get_barrier_semaphore()
    for peer in (zp, zm, yp, ym, *xpeer.values(), sib):
        pl.semaphore_signal(barrier, inc=1, device_id=peer, device_id_type=MESH)

    own = buf.at[0, xs, c, y]
    half = KV // 2
    loads = [
        pltpu.make_async_copy(src, dst, s_loc.at[i])
        for i, (src, dst) in enumerate((
            (w_hbm, own),
            (d_hbm, dbuf.at[zl, xx]),
            (grads_hbm, raw),
            (up_hbm, up),
            (x_hbm, xv),
            (gain_hbm, gain),
        ))
    ]
    for cp in loads:
        cp.start()

    def pieces(s):
        return pl.ds(0, 1) if s == 0 else (pl.ds(15, 1) if s == 8 else pl.ds(2 * s - 1, 2))

    def z_slot(s, direction):
        return 0 if s == 0 else (15 if s == 8 else 2 * s - 1 + direction)

    def z_send(s, direction, kind, part):
        start(
            buf.at[z_slot(s - 1, direction), part, c, y],
            buf.at[z_slot(s, direction), part, c, y],
            z_, r_z.at[direction, s, kind], zm if direction else zp,
        )

    def z_step(s, kind):
        half_ = xs if kind == 0 else 1 - xs
        for direction in (0, 1):
            arrived(buf.at[z_slot(s, direction), half_, c, y], r_z.at[direction, s, kind])
            if s < 7:
                z_send(s + 1, direction, kind, half_)
            else:
                pl.when(half_ == direction)(functools.partial(far_copy(direction).start))

    def far_copy(direction):
        return remote(
            buf.at[z_slot(7, direction), direction, c, y], buf.at[15, direction, c, y],
            z_, r_z8.at[direction], zm if direction else zp,
        )

    def in_line(s, direction):
        return zl >= s if direction == 0 else zl + s < ZL

    def more(direction):
        return zl < ZL - 1 if direction == 0 else zl > 0

    def d_copy(s, direction, row):
        ref = dbuf.at[row, xx]
        sent = dz1 if direction else dz0
        return remote(ref, ref, sent, r_dz.at[direction, s], zm if direction else zp)

    def d_pair(s, direction):
        row = zl - s if direction == 0 else zl + s
        ok = in_line(s, direction) & (row % 2 == direction)
        return ok, row // 2

    def d_across(g):
        for d in (1, 2, 3):
            ref = dbuf.at[pl.ds(2 * g, 2), xx]
            start(ref, ref, d_, r_d.at[g], xpeer[d])

    def d_step(s):
        for direction in (0, 1):

            def go(direction=direction):
                row = zl - s if direction == 0 else zl + s
                arrived(dbuf.at[row, xx], r_dz.at[direction, s])

                def forward():
                    d_copy(s, direction, row).wait_send()
                    if s < 7:
                        d_copy(s + 1, direction, row).start()

                pl.when(more(direction))(forward)

            pl.when(in_line(s, direction))(go)
            pl.when((zl == (s - 1 if direction == 0 else 8 - s)) & more(direction))(
                lambda: d_copy(s, direction, zl).wait_send()
            )
            ok, g = d_pair(s, direction)
            pl.when(ok)(functools.partial(d_across, g))

    def d_done(s):
        for direction in (0, 1):
            ok, g = d_pair(s, direction)

            def go(g=g):
                arrived(dbuf.at[pl.ds(2 * g, 2), 0:3], r_d.at[g])

                def add(i, acc):
                    row = 2 * g + i // 4
                    return acc + dot(scaled[8 * g + i], dbuf[row, i % 4], NT)

                lin[...] += lax.fori_loop(0, 8, add, jnp.zeros((T, R), F32), unroll=8)

            pl.when(ok)(go)

    both = pl.ds(0, 2)
    halves = (xs, 1 - xs)

    def y_send(s, kind):
        src = buf.at[pieces(s), halves[kind], c, y]
        for peer in (yp, ym):
            start(src, src, y1, r_y1.at[s, kind], peer)

    def y_send_far():
        src = buf.at[pieces(8), both, c, y]
        for peer in (yp, ym, yf):
            start(src, src, y2, r_y1.at[8, 0], peer)

    def z_whole(k):
        other = mod(y + k, NY)
        for direction, peer in ((0, zp), (1, zm)):
            start(
                buf.at[0, both, c, other], buf.at[1 + direction, both, c, other],
                yz, r_yz.at[direction], peer,
            )

    def y_relay(s, kind):
        half_ = halves[kind]
        arrived(buf.at[pieces(s), half_, c, 0:2], r_y1.at[s, kind])
        src = buf.at[pieces(s), half_, c, mod(y - 1 + 2 * half_, NY)]
        start(src, src, y2, r_y2.at[s], dev(z, mod(y + 1 - 2 * half_, NY), xx, c))

    def y_done(s):
        if s == 8:
            arrived(buf.at[pieces(s), both, c, 0:3], r_y1.at[s, 0])
        elif s == 1:
            for direction in (0, 1):
                arrived(buf.at[1 + direction, both, c, 0:3], r_yz.at[direction])
        else:
            arrived(buf.at[pieces(s), both, c, 0], r_y2.at[s])
        src = buf.at[pieces(s), both, c]
        start(src, src, sb, r_sib.at[s], sib)

    def sib_done(s):
        arrived(buf.at[pieces(s), both, 1 - c], r_sib.at[s])
        if s == 4:
            block(mod(zl + 4, ZL), 8, 7)
        elif s == 8:
            block(zl, 15, 0)
        elif s > 4:
            block(mod(zl + s, ZL), 2 * s, 15 - 2 * s)
            block(mod(zl - s, ZL), 2 * s - 1, 16 - 2 * s)

    def p_pairs(k):
        g = zl // 2
        if k == 4:
            return [(g >= 0, g)]
        return [(g + 4 - k < 4, g + 4 - k), (g - 4 + k >= 0, g - 4 + k)]

    def p_copy(d, g):
        return remote(
            part.at[mod(xx + d, NX), pl.ds(2 * g, 2)], part_in.at[d, pl.ds(2 * g, 2)],
            p_, r_p.at[g], xpeer[d],
        )

    def p_send(k):
        for ok, g in p_pairs(k):

            def go(g=g):
                def one(i, carry):
                    term = dot(lr_t, scaled[8 * g + i], NN)
                    part[i % 4, 2 * g + i // 4] = term.astype(BF16)
                    return carry

                lax.fori_loop(0, 8, one, 0, unroll=8)
                for d in (1, 2, 3):
                    p_copy(d, g).start()

            pl.when(ok)(go)

    def p_done(k):
        for ok, g in p_pairs(k):

            def go(g=g):
                arrived(part_in.at[1:4, pl.ds(2 * g, 2)], r_p.at[g])
                for i in (0, 1):
                    acc = part[xx, 2 * g + i].astype(F32)
                    for d in (1, 2, 3):
                        acc += part_in[d, 2 * g + i].astype(F32)
                    summed[2 * g + i] = acc

            pl.when(ok)(go)

    def c_copy(src, direction, j):
        return remote(
            src, chain.at[direction, j], c1 if direction else c0, r_c.at[direction, j],
            zm if direction else zp,
        )

    def c_step(j):
        for direction, place, row in ((0, zl, zl + 8 - j), (1, 7 - zl, zl - 8 + j)):

            def first(direction=direction, row=row):
                if j > 1:
                    c_copy(summed.at[0], direction, j - 1).wait_send()
                c_copy(summed.at[row], direction, j).start()

            pl.when(place == 0)(first)

            def later(direction=direction, place=place, row=row):
                here = chain.at[direction, j - 1]
                arrived(here, r_c.at[direction, j - 1])
                here[...] += summed[row]
                if j > 2:

                    @pl.when(place <= j - 2)
                    def _():
                        c_copy(here, direction, j - 1).wait_send()

                c_copy(here, direction, j).start()

            if j >= 2:
                pl.when((place >= 1) & (place <= j - 1))(later)

    def c_last():
        down[...] = summed[zl]
        for direction, place in ((0, zl), (1, 7 - zl)):

            def go(direction=direction):
                arrived(chain.at[direction, 7], r_c.at[direction, 7])
                down[...] += chain[direction, 7]

            pl.when(place >= 1)(go)
            pl.when(place <= 6)(
                functools.partial(c_copy(summed.at[0], direction, 7).wait_send)
            )
        pltpu.make_async_copy(down, down_out, s_loc.at[0]).start()

    def res_copy(n, row, p):
        tokens = pl.ds(64 * n, 64)
        return remote(
            res.at[row, :, pl.ds(T + 64 * n, 64)], fg.at[row, :, p, tokens], res_, r_res.at[row],
            xpeer[1 if n else 3],
        )

    def own_copy(row):
        return pltpu.make_async_copy(
            res.at[row, :, 0:T], fg.at[row, :, par], own_
        )

    def block(row, qa, qb):
        steps = (qa + 1) // 2
        first = (mod(z - steps, NZ) if qa % 2 else mod(z + steps, NZ)) // ZL

        def one(i, carry):
            acc = dot(tok[first], buf[qa, i].reshape(half, B), NN)
            acc += dot(tok[1 - first], buf[qb, i].reshape(half, B), NN)
            acc += dot(lr4[...], dbuf[row, par + 2 * i], NN)
            res[row, i] = acc.astype(BF16)
            return carry

        lax.fori_loop(0, 2, one, 0, unroll=2)
        for n in (0, 1):
            res_copy(n, row, par).start()
        own_copy(row).start()

    def core_major(values, h):
        blocks = [values[:, h * half + i * R:h * half + (i + 1) * R] for i in range(8)]
        return jnp.concatenate(blocks[0::2] + blocks[1::2], axis=1)

    def lowrank(rows):
        return (
            dot(tok[0, rows], up2[0], NT) + dot(tok[1, rows], up2[1], NT)
        ).astype(BF16)

    def pack_up():
        lb = lin[...].astype(BF16)
        for h in (0, 1):
            term = dot(tok[h, 0:T], lb, TN)
            term = term.reshape(2, NY, 2, 32, R).swapaxes(1, 2)
            upart[:, :, :, h * R:(h + 1) * R] = term.reshape(NX, 4, 32, R).astype(BF16)
        for d in (1, 2, 3):
            start(upart.at[mod(xx + d, NX)], upart_in.at[d], u_, r_u, xpeer[d])

    def up_over_z():
        acc = upart[xx].astype(F32)
        arrived(upart_in.at[1:4], r_u)
        for d in (1, 2, 3):
            acc += upart_in[d].astype(F32)
        for h in (0, 1):
            usum[4 * h:4 * h + 4] = acc[:, :, h * R:(h + 1) * R]
        for d in (4, 3, 5, 2, 6, 1, 7):
            row = mod(zl + d, ZL)
            start(usum.at[row], uin.at[d], uz, r_uz, dev(zh * ZL + row, y, xx, c))

    def up_last():
        acc = usum[zl]
        arrived(uin.at[1:8], r_uz)
        for d in range(1, 8):
            acc += uin[d]
        upg[...] = acc
        pltpu.make_async_copy(upg, up_out, s_loc.at[1]).start()

    def square(i, acc):
        v = xv[:, pl.ds(pl.multiple_of(i * B, B), B)].astype(F32)
        return acc + v * v

    def make_scaled(i, carry):
        columns = pl.ds(pl.multiple_of(i * B, B), B)
        scaled[i] = (xv[:, columns].astype(F32) * inv[...] * gain[:, columns]).astype(BF16)
        return carry

    for i in (0, 1):
        loads[i].wait()
    pl.semaphore_wait(barrier, 8)

    start(own, own, w2, r_w2, xpeer[2])
    for direction in (0, 1):
        z_send(1, direction, 0, xs)
    y_send(0, 0)
    for direction in (0, 1):
        pl.when(more(direction))(functools.partial(d_copy(1, direction, zl).start))
    loads[2].wait()
    for h in (0, 1):
        tok[h, 0:T] = core_major(raw[...], h)
    for n in (0, 1):
        start(
            tok.at[:, 64 * n:64 * n + 64], tok.at[:, T + 64 * n:T + 64 * n + 64],
            g_, r_g, xpeer[3 if n else 1],
        )
    loads[4].wait()
    total = lax.fori_loop(0, 32, square, jnp.zeros((T, B), F32), unroll=2)
    inv[...] = lax.rsqrt(jnp.sum(total, axis=1, keepdims=True) / D + norm_eps)

    arrived(buf.at[0, 1 - xs, c, y], r_w2)
    for direction in (0, 1):
        z_send(1, direction, 1, 1 - xs)
    y_send(0, 1)

    loads[3].wait()
    for h in (0, 1):
        up2[h] = core_major(up[...], h)
    lr_t = (dot(up2[0], tok[0, 0:T], NT) + dot(up2[1], tok[1, 0:T], NT)).astype(BF16)
    lr4[0:T] = lowrank(slice(0, T)) * adapter_scale
    lin[...] = jnp.zeros_like(lin)
    loads[5].wait()
    lax.fori_loop(0, 32, make_scaled, 0, unroll=2)
    p_send(1)

    d_done_at = {3: (1,), 4: (2,), 5: (3,), 6: (4,), 7: (5,)}
    p_done_at = {3: 1, 5: 2, 7: 3}
    y_done_at = {2: (0,), 5: (1, 2), 6: (3, 4), 7: (5,)}
    for s in range(1, 8):
        for kind in (0, 1):
            z_step(s, kind)
            if s > 1:
                y_send(s, kind)
        if s != 2:
            y_relay(s - 1, 0)
            y_relay(s - 1, 1)
        if s <= 6:
            d_step(s)
        for v in y_done_at.get(s, ()):
            y_done(v)
        if 2 <= s <= 4:
            z_whole(s - 1)
        if s == 1:
            arrived(tok.at[:, T:2 * T], r_g)
            lr4[T:] = lowrank(slice(T, 2 * T)) * adapter_scale
        if s in (1, 3, 5):
            p_send((s + 3) // 2)
        if s in p_done_at:
            p_done(p_done_at[s])
        if s >= 3:
            c_step(s - 2)
        for v in d_done_at.get(s, ()):
            d_done(v)
        if s == 6:
            d_step(7)

    y_relay(7, 0)
    y_relay(7, 1)
    for direction in (0, 1):
        arrived(buf.at[15, direction, c, y], r_z8.at[direction])
    y_send_far()
    y_done(6)
    c_step(6)
    p_done(4)
    d_done(6)
    d_done(7)
    pack_up()
    sib_done(4)
    sib_done(3)
    sib_done(5)
    y_done(7)
    y_done(8)
    up_over_z()
    sib_done(2)
    sib_done(6)
    c_step(7)
    sib_done(1)
    sib_done(7)
    sib_done(0)
    sib_done(8)
    c_last()
    up_last()
    with jax.named_scope("features_wait"):
        for row in range(ZL):
            arrived(fg.at[row, :, 1 - par], r_res.at[row])
    with jax.named_scope("sends_wait"):
        drained(own, w2)
        drained(tok.at[:, 0:T], g_)
        drained(buf.at[0:15, 0, 0, 0:2], z_)
        drained(buf.at[0:13, 0, 0], y1)
        drained(buf.at[0:16, 0, 0, 0:2], y2)
        drained(buf.at[0:3, 0, 0], yz)
        drained(buf.at[0:16, 0:2, 0], sb)
        drained(dbuf.at[:, 0:3], d_)
        drained(part.at[0:3], p_)
        drained(res.at[:, 0:1], res_)
        drained(upart.at[1:4], u_)
        drained(usum.at[1:8], uz)
        pltpu.make_async_copy(res.at[:, :, 0:T], fg.at[:, :, par], own_).wait()
        pltpu.make_async_copy(down, down_out, s_loc.at[0]).wait()
        pltpu.make_async_copy(upg, up_out, s_loc.at[1]).wait()


def exchange(x, grads, w, d, up, gain):
    sem = pltpu.SemaphoreType.DMA
    hbm = pl.BlockSpec(memory_space=pl.ANY)
    return pl.pallas_call(
        main_kernel,
        out_shape=(
            jax.ShapeDtypeStruct((ZL, 2, 2, T, B), BF16),
            jax.ShapeDtypeStruct((R, B), F32),
            jax.ShapeDtypeStruct((32, R), F32),
        ),
        in_specs=[hbm] * 6,
        out_specs=(hbm, hbm, hbm),
        scratch_shapes=[
            pltpu.VMEM((T, D), BF16),
            pltpu.VMEM((T, KV), BF16),
            pltpu.VMEM((R, KV), BF16),
            pltpu.VMEM((2, R, KV // 2), BF16),
            pltpu.VMEM((1, D), F32),
            pltpu.VMEM((32, T, B), BF16),
            pltpu.VMEM((16, 2, 2, NY, R, B), BF16),
            pltpu.VMEM((ZL, NX, R, B), BF16),
            pltpu.VMEM((2, 2 * T, KV // 2), BF16),
            pltpu.VMEM((2 * T, R), BF16),
            pltpu.VMEM((ZL, 2, 2 * T, B), BF16),
            pltpu.VMEM((T, 1), F32),
            pltpu.VMEM((NX, ZL, R, B), BF16),
            pltpu.VMEM((NX, ZL, R, B), BF16),
            pltpu.VMEM((ZL, R, B), F32),
            pltpu.VMEM((2, 8, R, B), F32),
            pltpu.VMEM((T, R), F32),
            pltpu.VMEM((NX, ZL // 2, 32, 2 * R), BF16),
            pltpu.VMEM((NX, ZL // 2, 32, 2 * R), BF16),
            pltpu.VMEM((ZL, 32, R), F32),
            pltpu.VMEM((ZL, 32, R), F32),
            pltpu.VMEM((R, B), F32),
            pltpu.VMEM((32, R), F32),
            sem((6,)),
            sem((17,)),
            sem((2,)),
            sem((4,)),
            sem((2, 8, 2)),
            sem((2,)),
            sem((2, 8)),
            sem((9, 2)),
            sem((9,)),
            sem((9,)),
            sem((4,)),
            sem((4,)),
            sem((2, 8)),
            sem((8,)),
        ],
        compiler_params=pltpu.CompilerParams(
            collective_id=1, has_side_effects=True, vmem_limit_bytes=60 << 20
        ),
        name="exchange",
    )(x, grads, w, d, up, gain)


def finish_kernel(scaling, x, fg, gain, down, up, out, down_out, up_out):
    @pl.when(pl.program_id(0) == 0)
    def _():
        down_out[...] = scaling * down[...]
        up_out[...] = scaling * up[...]

    rows = x.shape[0]
    squares = jnp.zeros((rows, B), F32)
    products = jnp.zeros((rows, B), F32)
    for i in range(32):
        v = x[:, i * B:(i + 1) * B].astype(F32)
        g = fg[i // 4, (i % 4) // 2, i % 2].astype(F32) * gain[:, i * B:(i + 1) * B]
        squares += v * v
        products += v * g
    inv = lax.rsqrt(jnp.sum(squares, axis=1, keepdims=True) / D + norm_eps)
    slope = inv * inv * (jnp.sum(products, axis=1, keepdims=True) / D)
    for i in range(32):
        v = x[:, i * B:(i + 1) * B].astype(F32)
        g = fg[i // 4, (i % 4) // 2, i % 2].astype(F32) * gain[:, i * B:(i + 1) * B]
        out[:, i * B:(i + 1) * B] = (inv * (g - v * slope)).astype(BF16)


def finish(x, fg, gain, down, up, scaling):
    rows = 64

    def whole(*shape):
        return pl.BlockSpec(shape, lambda i: (0,) * len(shape))

    return pl.pallas_call(
        functools.partial(finish_kernel, scaling),
        grid=(T // rows,),
        out_shape=(
            jax.ShapeDtypeStruct((T, D), BF16),
            jax.ShapeDtypeStruct((R, B), F32),
            jax.ShapeDtypeStruct((32, R), F32),
        ),
        in_specs=[
            pl.BlockSpec((rows, D), lambda i: (i, 0)),
            pl.BlockSpec((ZL, 2, 2, rows, B), lambda i: (0, 0, 0, i, 0)),
            whole(1, D), whole(R, B), whole(32, R),
        ],
        out_specs=(pl.BlockSpec((rows, D), lambda i: (i, 0)), whole(R, B), whole(32, R)),
        compiler_params=pltpu.CompilerParams(vmem_limit_bytes=60 << 20),
        name="finish",
    )(x, fg, gain, down, up)


def per_device(layer_input, value_grads, value_weight, adapter_down, adapter_up, norm_gain):
    scaling = gradient_scale / math.sqrt(layer_input.shape[1] * lax.axis_size("tensor"))
    gain = norm_gain.reshape(1, D)
    fg, down_t, up_t = exchange(
        layer_input[0], value_grads[0], value_weight.T, adapter_down[0].T, adapter_up[0], gain
    )
    input_grads, down_grads, up_grads = finish(
        layer_input[0], fg, gain, down_t, up_t, scaling
    )
    return (input_grads[None], down_grads.T[None], up_grads.T[None])


def solution(mesh):
    return jax.shard_map(
        per_device,
        mesh=mesh,
        in_specs=(
            P("member", "tensor", None),
            P("member", "tensor", None),
            P("tensor", "member"),
            P("member", "tensor", None),
            P("member", None, None),
            P(),
        ),
        out_specs=(
            P("member", "tensor", None),
            P("member", "tensor", None),
            P("member", None, "tensor"),
        ),
        check_vma=False,
    )
```
